32 devices in a mesh: tgt: 4 (over y, core), src: 8 (over z, x).
Axes of the slice: x: 2, y: 2, z: 4, core: 2. Of those that a mesh axis runs over, the one named last changes fastest.
Arguments:
- shear_leaves: bfloat16 [8, 8, 128, 128], P('tgt', 'src'), may hold values from -2 to 2, as said below
- normal_leaves: bfloat16 [8, 8, 128, 128], P('tgt', 'src'), may hold values from -2 to 2, as said below
- near_flags: int32 [8, 8], P('tgt', 'src'), may hold values from 0 to 1, as said below
- ranks: int32 [8, 8], P('tgt', 'src'), may hold values from 16 to 64
- shear_traction: float32 [1024, 128], P(('tgt', 'src')), may hold values from -1 to 1
- normal_traction: float32 [1024, 128], P(('tgt', 'src')), may hold values from 0.5 to 4
- state: float32 [1024, 128], P(('tgt', 'src')), may hold values from -0.5 to 0.5
- friction_a: float32 [1024, 128], P(('tgt', 'src')), may hold values from 1 to 2
- heal_rate: float32 [1024, 128], P(('tgt', 'src')), may hold values from 0.1 to 0.5
Outputs:
- shear_out: float32 [1024, 128], P(('tgt', 'src'))
- normal_out: float32 [1024, 128], P(('tgt', 'src'))
- state_out: float32 [1024, 128], P(('tgt', 'src'))
The draws below stay inside these ranges and needn't reach their ends.
Inputs may be any that keep to these rules, and one draw needn't show every extreme that they name: `near_flags`: every leaf with equal leaf row and leaf column is 1, and a 1 stands only where the leaf row and the leaf column differ by at most 1. `shear_leaves`: columns 0 to 63 of an admissible leaf hold its factor U, columns 64 onward its factor V. `normal_leaves`: columns 0 to 63 of an admissible leaf hold its factor U, columns 64 onward its factor V.
All inputs are finite; a program needn't handle non-finite values.
Results may differ from the reference program's by a relative error of at most 0.002.
Values may be sent and summed in bfloat16 or wider, within the bound.
No kernel may reach another device: no remote copies, remote signals or barrier semaphores. Data moves between devices by JAX's collectives and lax.ppermute only.
A program may use at most 64 MiB of HBM per device.

```python
import math
import jax
import jax.numpy as jnp
from jax import lax

RMAX = 64
BLK = 128
NV = 128
LEAVES = 8
ELEMENTS = 1024


def leaf_pattern(key):
    coin_bits = jax.random.randint(jax.random.fold_in(key, 7), (LEAVES, LEAVES), 0, 2)
    row_ids = jnp.arange(LEAVES, dtype=jnp.int32)[:, None]
    col_ids = jnp.arange(LEAVES, dtype=jnp.int32)[None, :]
    spacing = jnp.abs(row_ids - col_ids)
    chosen = (spacing == 0) | (spacing == 1) & (coin_bits == 1)
    return jnp.where(chosen, 1, 0).astype(jnp.int32)


def leaf_values(key, salt, self_term):
    pattern = leaf_pattern(key)
    shape = (LEAVES, LEAVES, BLK, BLK)
    raw = jax.random.normal(jax.random.fold_in(key, salt), shape, jnp.float32)
    dense_scale = 0.5 / math.sqrt(BLK)
    factor_scale = (2.25 / (RMAX * BLK * LEAVES)) ** 0.25
    scaling = jnp.where(pattern[:, :, None, None] == 1, dense_scale, factor_scale).astype(jnp.float32)
    same_leaf = (jnp.arange(LEAVES)[:, None] == jnp.arange(LEAVES)[None, :]).astype(jnp.float32)
    values = raw * scaling + self_term * same_leaf[:, :, None, None] * jnp.eye(BLK, dtype=jnp.float32)[None, None]
    return values.astype(jnp.bfloat16)


def draw_near_flags(key, part):
    return leaf_pattern(key)


def draw_shear_leaves(key, part):
    return leaf_values(key, 21, -1.0)


def draw_normal_leaves(key, part):
    return leaf_values(key, 22, 0.0)


def set_ends(array, own_key, least, top_value):
    longest = array.shape.index(max(array.shape))
    spots = []
    for shift in (0, 1):
        where = [jax.random.randint(jax.random.fold_in(own_key, axis), (), 0, length) for axis, length in enumerate(array.shape)]
        where[longest] = (where[longest] + shift) % array.shape[longest]
        spots.append(tuple(where))
    return array.at[spots[0]].set(least).at[spots[1]].set(top_value)


def level_of(rng, extent, split, smallest, top_value):
    def one(dim, blocks):
        draws = jax.random.uniform(jax.random.fold_in(jax.random.fold_in(rng, 6), dim), (blocks,), jnp.float32, smallest / len(split), top_value / len(split))
        return jnp.repeat(jnp.exp(draws), extent[dim] // blocks).reshape((-1,) + (1,) * (len(extent) - dim - 1))

    level = one(*split[0])
    for cut in split[1:]:
        level = level * one(*cut)
    return level


def setup_inputs(seed: int = 0) -> dict:
    key_of = jax.random.split(jax.random.key(seed), 10)
    return {
        "shear_leaves": draw_shear_leaves(jax.random.fold_in(key_of[9], 71), 0),
        "normal_leaves": draw_normal_leaves(jax.random.fold_in(key_of[9], 71), 0),
        "near_flags": draw_near_flags(jax.random.fold_in(key_of[9], 71), 0),
        "ranks": set_ends(jax.random.randint(key_of[3], (LEAVES, LEAVES), RMAX // 4, RMAX + 1), jax.random.fold_in(key_of[3], 1), RMAX // 4, RMAX).astype(jnp.int32),
        "shear_traction": jnp.clip(jax.random.uniform(key_of[4], (ELEMENTS, NV), jnp.float32, -1.0, 1.0) * level_of(key_of[4], (ELEMENTS, NV), ((0, 32),), -0.4, 0.0), -1.0, 1.0),
        "normal_traction": jnp.clip(jnp.exp(math.log(4.0) - 2.0794415 * jax.random.uniform(key_of[5], (ELEMENTS, NV), jnp.float32) ** level_of(key_of[5], (ELEMENTS, NV), ((0, 32),), -0.2, 0.2)), 0.5, 4.0),
        "state": jnp.clip(jax.random.uniform(key_of[6], (ELEMENTS, NV), jnp.float32, -0.5, 0.5) * level_of(key_of[6], (ELEMENTS, NV), ((0, 32),), -0.4, 0.0), -0.5, 0.5),
        "friction_a": jnp.clip(jnp.exp(math.log(2.0) - 0.6931472 * jax.random.uniform(key_of[7], (ELEMENTS, NV), jnp.float32) ** level_of(key_of[7], (ELEMENTS, NV), ((0, 32),), -0.2, 0.2)), 1.0, 2.0),
        "heal_rate": jnp.clip(jnp.exp(math.log(0.5) - 1.609438 * jax.random.uniform(key_of[8], (ELEMENTS, NV), jnp.float32) ** level_of(key_of[8], (ELEMENTS, NV), ((0, 32),), -0.2, 0.2)), 0.1, 0.5),
    }


time_step = 0.25


def apply_kernel(leaves, near_flags, ranks, deviation):
    blocks = deviation.reshape(LEAVES, BLK, NV).astype(jnp.float32)
    rank_ids = jnp.arange(RMAX, dtype=jnp.int32)

    def one_row(item):
        leaf_row, near_row, rank_row, row_id = item
        columns = row_id + jnp.arange(3, dtype=jnp.int32) - 1
        valid = (columns >= 0) & (columns < LEAVES)
        safe_cols = jnp.clip(columns, 0, LEAVES - 1).astype(jnp.int32)
        band_leaves = leaf_row[safe_cols].astype(jnp.float32)
        band_blocks = blocks[safe_cols]
        band_near = (near_row[safe_cols] == 1) & valid
        dense = jnp.einsum("bij,bjn->bin", band_leaves, band_blocks)
        dense = jnp.sum(jnp.where(band_near[:, None, None], dense, 0.0), axis=0)
        factor_v = leaf_row[:, :, RMAX:].astype(jnp.float32)
        factor_u = leaf_row[:, :, :RMAX].astype(jnp.float32)
        inner = jnp.einsum("bjk,bjn->bkn", factor_v, blocks)
        keep_mask = (rank_ids[None, :] < rank_row[:, None]) & (near_row[:, None] == 0)
        inner = jnp.where(keep_mask[:, :, None], inner, 0.0).astype(jnp.bfloat16)
        inner = lax.optimization_barrier(inner).astype(jnp.float32)
        lowrank = jnp.einsum("bik,bkn->in", factor_u, inner)
        return dense + lowrank

    row_ids = jnp.arange(LEAVES, dtype=jnp.int32)
    result = lax.map(one_row, (leaves, near_flags, ranks, row_ids))
    return result.reshape(LEAVES * BLK, NV)


def reference(shear_leaves, normal_leaves, near_flags, ranks, shear_traction, normal_traction, state, friction_a, heal_rate):
    def rates(shear_now, normal_now, state_now):
        effective = jnp.maximum(normal_now, 1.0)
        slip_rate = 2.0 * jnp.exp(-state_now / friction_a) * jnp.sinh(shear_now / (friction_a * effective))
        deviation = (slip_rate - 1.0).astype(jnp.bfloat16)
        shear_rate = apply_kernel(shear_leaves, near_flags, ranks, deviation)
        normal_rate = apply_kernel(normal_leaves, near_flags, ranks, deviation)
        state_rate = heal_rate * (jnp.exp(-state_now) - slip_rate)
        return shear_rate, normal_rate, state_rate

    start = (shear_traction, normal_traction, state)
    first_rates = rates(*start)
    first = tuple(value + time_step * change for value, change in zip(start, first_rates))
    second_rates = rates(*first)
    second = tuple(0.75 * begin + 0.25 * (value + time_step * change) for begin, value, change in zip(start, first, second_rates))
    third_rates = rates(*second)
    third = tuple(begin / 3.0 + (2.0 / 3.0) * (value + time_step * change) for begin, value, change in zip(start, second, third_rates))
    return third[0], third[1], third[2]
```

```python
import functools

import jax
import jax.numpy as jnp
from jax import lax
from jax.experimental import pallas as pl
from jax.experimental.pallas import tpu as pltpu
from jax.sharding import PartitionSpec as P

time_step = 0.25
VMEM = pl.BlockSpec(memory_space=pltpu.VMEM)


def friction(shear_now, normal_now, state_now, friction_a):
    drive = shear_now / (friction_a * jnp.maximum(normal_now, 1.0))
    decay = state_now / friction_a
    return jnp.exp(drive - decay) - jnp.exp(-drive - decay)


def send_copies(dev_ref, slip_rate):
    deviation = (slip_rate - 1.0).astype(jnp.bfloat16)
    dev_ref[...] = jnp.broadcast_to(deviation[None], dev_ref.shape)


def prepare_kernel(near_ref, rank_ref, shear_ref, normal_ref, s_ref, n_ref, p_ref, a_ref, strips_ref, dev_ref):
    leaf_rows, leaf_cols, block, _ = shear_ref.shape
    half = block // 2
    own = s_ref.shape[0]
    rank_ids = lax.broadcasted_iota(jnp.int32, (block, half), 1)
    per_leaf = block // own
    for row in range(leaf_rows):
        for col in range(leaf_cols):
            near = near_ref[row : row + 1, col : col + 1] == 1
            for which, leaves in enumerate((shear_ref, normal_ref)):
                leaf = leaves[row, col]
                factor_u = jnp.where(rank_ids < rank_ref[row : row + 1, col : col + 1], leaf[:, :half].astype(jnp.float32), 0.0)
                product = lax.dot_general(
                    factor_u.astype(jnp.bfloat16),
                    leaf[:, half:],
                    (((1,), (1,)), ((), ())),
                    preferred_element_type=jnp.float32,
                )
                dense = jnp.where(near, leaf.astype(jnp.float32), product).astype(jnp.bfloat16)
                for part in range(per_leaf):
                    strips_ref[row * per_leaf + part, which * own : (which + 1) * own, col * block : (col + 1) * block] = (
                        dense[part * own : (part + 1) * own]
                    )
    send_copies(dev_ref, friction(s_ref[...], n_ref[...], p_ref[...], a_ref[...]))


def stage_kernel(stage, strips_ref, all_dev_ref, *refs):
    if stage == 0:
        s0_ref, n0_ref, p0_ref, a_ref, h_ref = refs[:5]
        begin = now = (s0_ref[...], n0_ref[...], p0_ref[...])
        outs = refs[5:]
    else:
        s0_ref, n0_ref, p0_ref, a_ref, h_ref, s_ref, n_ref, p_ref = refs[:8]
        begin = (s0_ref[...], n0_ref[...], p0_ref[...])
        now = (s_ref[...], n_ref[...], p_ref[...])
        outs = refs[8:]
    friction_a = a_ref[...]
    own = friction_a.shape[0]
    pieces, _, width = strips_ref.shape
    total = jnp.zeros((2 * own, friction_a.shape[1]), jnp.float32)
    for piece in range(pieces):
        total += jnp.dot(
            strips_ref[piece], all_dev_ref[piece * width : (piece + 1) * width], preferred_element_type=jnp.float32
        )
    slip_rate = friction(*now, friction_a)
    rates = (total[:own], total[own:], h_ref[...] * (jnp.exp(-now[2]) - slip_rate))
    moved = tuple(value + time_step * change for value, change in zip(now, rates))
    if stage == 1:
        moved = tuple(0.75 * start + 0.25 * value for start, value in zip(begin, moved))
    elif stage == 2:
        moved = tuple(start / 3.0 + (2.0 / 3.0) * value for start, value in zip(begin, moved))
    for out, value in zip(outs, moved):
        out[...] = value
    if stage < 2:
        send_copies(outs[3], friction(*moved, friction_a))


def per_device(
    shear_leaves, normal_leaves, near_flags, ranks, shear_traction, normal_traction, state, friction_a, heal_rate
):
    leaf_rows, leaf_cols, block, _ = shear_leaves.shape
    own, members = state.shape
    sources = lax.axis_size("src")
    devices = sources * lax.axis_size("tgt")
    row_type = jax.ShapeDtypeStruct((own, members), jnp.float32)
    copies_type = jax.ShapeDtypeStruct((devices, own, members), jnp.bfloat16)

    strips, copies = pl.pallas_call(
        prepare_kernel,
        out_shape=(jax.ShapeDtypeStruct((sources, 2 * own, leaf_cols * block), jnp.bfloat16), copies_type),
        in_specs=[VMEM] * 8,
        out_specs=(VMEM, VMEM),
    )(near_flags, ranks, shear_leaves, normal_leaves, shear_traction, normal_traction, state, friction_a)
    strips = lax.all_to_all(strips, "src", 0, 0, tiled=True)

    begin = (shear_traction, normal_traction, state)
    now = ()
    for stage in range(3):
        all_dev = lax.all_to_all(copies, ("tgt", "src"), 0, 0, tiled=True).reshape(devices * own, members)
        given = (strips, all_dev, *begin, friction_a, heal_rate, *now)
        outs = pl.pallas_call(
            functools.partial(stage_kernel, stage),
            out_shape=(row_type,) * 3 + ((copies_type,) if stage < 2 else ()),
            in_specs=[VMEM] * len(given),
            out_specs=(VMEM,) * (4 if stage < 2 else 3),
        )(*given)
        now = outs[:3]
        if stage < 2:
            copies = outs[3]
    return tuple(now)


def solution(mesh):
    rows = P(("tgt", "src"), None)
    leaves = P("tgt", "src", None, None)
    flags = P("tgt", "src")
    return jax.shard_map(
        per_device,
        mesh=mesh,
        in_specs=(leaves, leaves, flags, flags) + (rows,) * 5,
        out_specs=(rows,) * 3,
        check_vma=False,
    )
```

```python
import functools

import jax
import jax.numpy as jnp
from jax import lax
from jax.experimental import pallas as pl
from jax.experimental.pallas import tpu as pltpu
from jax.sharding import PartitionSpec as P

time_step = 0.25
VMEM = pl.BlockSpec(memory_space=pltpu.VMEM)


def partner(index, step, count):
    return index ^ step if count & (count - 1) == 0 else (index + step) % count


def origin(index, step, count):
    return index ^ step if count & (count - 1) == 0 else (index + count - step) % count


def pair_of(sources):
    return 2 if sources % 2 == 0 else 1


def block_order(me, sources):
    pair = pair_of(sources)
    line = sources // pair
    far, near = me // pair, me % pair
    return [
        origin(far, step, line) * pair + origin(near, side, pair) for side in range(pair) for step in range(line)
    ]


def along_line(block, step):
    sources = lax.axis_size("src")
    pair = pair_of(sources)
    line = sources // pair
    moves = [(i, partner(i // pair, step, line) * pair + i % pair) for i in range(sources)]
    return lax.ppermute(block, "src", moves)


def across_pair(block):
    return lax.ppermute(block, "src", [(i, i ^ 1) for i in range(lax.axis_size("src"))])


def gather_source(block):
    sources = lax.axis_size("src")
    pair = pair_of(sources)
    blocks = [block] + [along_line(block, step) for step in range(1, sources // pair)]
    return blocks + ([across_pair(held) for held in blocks] if pair == 2 else [])


def gather_target(block):
    targets = lax.axis_size("tgt")
    return [block] + [
        lax.ppermute(block, "tgt", [(i, partner(i, step, targets)) for i in range(targets)])
        for step in range(1, targets)
    ]


def friction(shear_now, normal_now, state_now, friction_a):
    drive = shear_now / (friction_a * jnp.maximum(normal_now, 1.0))
    decay = state_now / friction_a
    return jnp.exp(drive - decay) - jnp.exp(-drive - decay)


def deviation_of(slip_rate):
    return (slip_rate - 1.0).astype(jnp.bfloat16)


def lane_side(shape, half):
    return lax.broadcasted_iota(jnp.int32, shape, len(shape) - 1) // half


def pack_kernel(*refs):
    packed_ref = refs[-1]
    own = refs[0].shape[0]
    for i, ref in enumerate(refs[:-1]):
        packed_ref[i * own : (i + 1) * own] = ref[...]


def dense_kernel(near_ref, rank_ref, shear_ref, normal_ref, dense_ref):
    leaf_rows, leaf_cols, block, _ = shear_ref.shape
    half = block // 2
    rank_ids = lax.broadcasted_iota(jnp.int32, (block, half), 1)
    for which, leaves in enumerate((shear_ref, normal_ref)):
        for row in range(leaf_rows):
            for col in range(leaf_cols):
                near = near_ref[col : col + 1, row : row + 1] == 1
                leaf = leaves[row, col]
                kept = rank_ids < rank_ref[col : col + 1, row : row + 1]
                factor_u = jnp.where(kept, leaf[:, :half].astype(jnp.float32), 0.0).astype(jnp.bfloat16)
                product = lax.dot_general(
                    factor_u, leaf[:, half:], (((1,), (1,)), ((), ())), preferred_element_type=jnp.float32
                )
                dense = jnp.where(near, leaf.astype(jnp.float32), product).astype(jnp.bfloat16)
                start = (which * leaf_rows + row) * block
                dense_ref[start : start + block, col * block : (col + 1) * block] = dense


def join_kernel(mine_ref, theirs_ref, *outs):
    half = mine_ref.shape[1] // 2
    side = lax.axis_index("src") % 2
    theirs = pltpu.roll(theirs_ref[...], half, 1)
    joined = jnp.where(lane_side(theirs.shape, half) == side, mine_ref[...], theirs)
    each = joined.shape[0] // len(outs)
    for i, out in enumerate(outs):
        out[...] = joined[i * each : (i + 1) * each]


def unpack_kernel(count, *refs):
    blocks, outs, dev_ref = refs[: -count - 1], refs[-count - 1 : -1], refs[-1]
    own = blocks[0].shape[0] // count
    far = lax.axis_index("src") // 2
    for step, block in enumerate(blocks):
        start = pl.multiple_of(origin(far, step, len(blocks)) * own, own)
        for i, out in enumerate(outs):
            out[pl.ds(start, own)] = block[i * own : (i + 1) * own]
    dev_ref[...] = deviation_of(friction(*(out[...] for out in outs[:4])))


def stage_kernel(stage, own, dense_count, targets, *refs):
    refs, all_dev = refs[:-1], refs[-1]
    dense_in, refs = refs[:dense_count], refs[dense_count:]
    dev_in, refs = refs[:targets], refs[targets:]
    begin_in, (a_ref, h_ref), refs = refs[:3], refs[3:5], refs[5:]
    now_in, outs = (refs[:3], refs[3:]) if stage else (begin_in, refs)

    joined, members = dev_in[0].shape
    half = members // 2
    rows, line = 2 * joined, joined // own
    for step, dev_ref in enumerate(dev_in):
        place = origin(lax.axis_index("tgt"), step, targets) * rows
        dev = dev_ref[...].astype(jnp.float32)
        for side, part in enumerate((dev, pltpu.roll(dev, half, 1))):
            for far in range(line):
                start = pl.multiple_of(place + (2 * far + side) * own, own)
                all_dev[pl.ds(start, own)] = part[far * own : (far + 1) * own]
    deviations = all_dev[...].astype(jnp.bfloat16)
    if stage == 0:
        dense_ref, outs = outs[-1], outs[:-1]
        width = dense_in[0].shape[1]
        for place, dense in zip(block_order(lax.axis_index("src"), dense_count), dense_in):
            dense_ref[:, pl.ds(pl.multiple_of(place * width, width), width)] = dense[...]
    else:
        dense_ref = dense_in[0]

    if stage < 2:
        mine, kept = slice(None), line
        total = jnp.dot(dense_ref[...], deviations, preferred_element_type=jnp.float32)
        totals = [total[:rows], total[rows:]]
    else:
        kept = 1
        far = lax.axis_index("src") // 2
        mine = pl.ds(pl.multiple_of(far * own, own), own)
        start = pl.multiple_of(far * 2 * own, 2 * own)
        totals = [
            jnp.dot(dense_ref[pl.ds(first + start, 2 * own)], deviations, preferred_element_type=jnp.float32)
            for first in (0, rows)
        ]
    change = []
    for total in totals:
        sides = [
            jnp.concatenate([total[(2 * far + side) * own : (2 * far + side + 1) * own] for far in range(kept)])
            for side in range(2)
        ]
        change.append(
            jnp.where(lane_side(sides[0].shape, half) == 0, sides[0], pltpu.roll(sides[1], half, 1))
        )
    now = tuple(ref[mine] for ref in now_in)
    friction_a = a_ref[mine]
    change.append(h_ref[mine] * (jnp.exp(-now[2]) - friction(*now, friction_a)))
    moved = tuple(value + time_step * rate for value, rate in zip(now, change))
    if stage:
        begin = tuple(ref[mine] for ref in begin_in)
    if stage == 1:
        moved = tuple(0.75 * first + 0.25 * value for first, value in zip(begin, moved))
    elif stage == 2:
        moved = tuple(first / 3.0 + (2.0 / 3.0) * value for first, value in zip(begin, moved))
        for i, value in enumerate(moved):
            outs[0][i * own : (i + 1) * own] = value
        return
    for out, value in zip(outs, moved):
        out[...] = value
    outs[3][...] = deviation_of(friction(*moved, friction_a))


def call(kernel, outs, given, scratch=(), limit=48 << 20):
    return pl.pallas_call(
        kernel,
        out_shape=tuple(outs),
        in_specs=[VMEM] * len(given),
        out_specs=(VMEM,) * len(outs),
        scratch_shapes=list(scratch),
        compiler_params=pltpu.CompilerParams(vmem_limit_bytes=limit),
    )(*given)


def per_device(
    shear_leaves, normal_leaves, near_flags, ranks, shear_traction, normal_traction, state, friction_a, heal_rate
):
    leaf_rows, leaf_cols, block, _ = shear_leaves.shape
    own, members = state.shape
    sources, targets = lax.axis_size("src"), lax.axis_size("tgt")
    rows = own * sources
    arrays = (shear_traction, normal_traction, state, friction_a, heal_rate)

    def floats(count):
        return jax.ShapeDtypeStruct((count, members), jnp.float32)

    wide = floats(rows // 2)
    dev_type = jax.ShapeDtypeStruct((rows // 2, members), jnp.bfloat16)

    (packed,) = call(pack_kernel, (floats(len(arrays) * own),), arrays, limit=60 << 20)
    (dense,) = call(
        dense_kernel,
        (jax.ShapeDtypeStruct((2 * rows, leaf_cols * block), jnp.bfloat16),),
        (near_flags.T, ranks.T, shear_leaves, normal_leaves),
        limit=60 << 20,
    )
    (joined,) = call(join_kernel, (floats(len(arrays) * own),), (packed, across_pair(packed)))
    joined_blocks = [joined] + [along_line(joined, step) for step in range(1, sources // 2)]
    dense_blocks = gather_source(dense)
    *begin, all_a, all_h, dev = call(
        functools.partial(unpack_kernel, len(arrays)), (wide,) * len(arrays) + (dev_type,), joined_blocks
    )
    now = ()
    matrix_type = jax.ShapeDtypeStruct((2 * rows, sources * leaf_cols * block), jnp.bfloat16)
    for stage in range(3):
        given = (*dense_blocks, *gather_target(dev), *begin, all_a, all_h, *now)
        outs = ((wide,) * 3 + (dev_type,)) if stage < 2 else (floats(3 * own),)
        outs = outs + ((matrix_type,) if stage == 0 else ())
        results = call(
            functools.partial(stage_kernel, stage, own, len(dense_blocks), targets),
            outs,
            given,
            [pltpu.VMEM((rows * targets, members), jnp.float32)],
        )
        now = results[:3]
        if stage < 2:
            dev = results[3]
        if stage == 0:
            dense_blocks = [results[4]]
    return call(join_kernel, (floats(own),) * 3, (results[0], across_pair(results[0])))


def solution(mesh):
    rows = P(("tgt", "src"), None)
    leaves = P("tgt", "src", None, None)
    flags = P("tgt", "src")
    return jax.shard_map(
        per_device,
        mesh=mesh,
        in_specs=(leaves, leaves, flags, flags) + (rows,) * 5,
        out_specs=(rows,) * 3,
        check_vma=False,
    )
```

```python
import functools

import jax
import jax.numpy as jnp
from jax import lax
from jax.experimental import pallas as pl
from jax.experimental.pallas import tpu as pltpu
from jax.sharding import PartitionSpec as P

time_step = 0.25
PAIR = 2
VMEM = pl.BlockSpec(memory_space=pltpu.VMEM)
HBM = pl.BlockSpec(memory_space=pltpu.HBM)


def partner(index, step, count):
    return index ^ step if count & (count - 1) == 0 else (index + step) % count


def origin(index, step, count):
    return index ^ step if count & (count - 1) == 0 else (index + count - step) % count


def block_order(me, sources):
    line = sources // PAIR
    return [origin(me // PAIR, step, line) * PAIR + (me % PAIR ^ side) for side in range(PAIR) for step in range(line)]


def along_line(block, step):
    sources = lax.axis_size("src")
    moves = [(i, partner(i // PAIR, step, sources // PAIR) * PAIR + i % PAIR) for i in range(sources)]
    return lax.ppermute(block, "src", moves)


def across_pair(block):
    return lax.ppermute(block, "src", [(i, i ^ 1) for i in range(lax.axis_size("src"))])


def gather_line(block, ready=()):
    line = lax.axis_size("src") // PAIR
    blocks = [block]
    for step in range(1, line):
        low = step & -step
        if line & (line - 1) or step == low:
            blocks.append(along_line(block, step))
        else:
            held, *_ = lax.optimization_barrier((blocks[step ^ low], *ready))
            blocks.append(along_line(held, low))
    return blocks


def gather_target(block):
    targets = lax.axis_size("tgt")
    return [block] + [
        lax.ppermute(block, "tgt", [(i, partner(i, step, targets)) for i in range(targets)])
        for step in range(1, targets)
    ]


def friction(shear_now, normal_now, state_now, friction_a):
    drive = shear_now / (friction_a * jnp.maximum(normal_now, 1.0))
    decay = state_now / friction_a
    return jnp.exp(drive - decay) - jnp.exp(-drive - decay)


def deviation_of(slip_rate):
    return (slip_rate - 1.0).astype(jnp.bfloat16)


def lane_side(shape, half):
    return lax.broadcasted_iota(jnp.int32, shape, len(shape) - 1) // half


def prepare_kernel(*refs):
    given, (packed_ref, dense_ref), held, sems = refs[:9], refs[9:11], refs[11:15], refs[15]
    own = given[4].shape[0]
    copies = [pltpu.make_async_copy(ref, place, sems.at[i]) for i, (ref, place) in enumerate(zip(given, held))]
    copies += [
        pltpu.make_async_copy(ref, packed_ref.at[pl.ds(i * own, own)], sems.at[4 + i])
        for i, ref in enumerate(given[4:])
    ]
    for copy in copies:
        copy.start()
    for copy in copies:
        copy.wait()
    near_ref, rank_ref, shear_ref, normal_ref = held
    leaf_rows, leaf_cols, block, _ = shear_ref.shape
    half = block // 2
    rank_ids = lax.broadcasted_iota(jnp.int32, (block, half), 1)
    for which, leaves in enumerate((shear_ref, normal_ref)):
        for row in range(leaf_rows):
            for col in range(leaf_cols):
                near = near_ref[col : col + 1, row : row + 1] == 1
                leaf = leaves[row, col]
                kept = rank_ids < rank_ref[col : col + 1, row : row + 1]
                factor_u = jnp.where(kept, leaf[:, :half].astype(jnp.float32), 0.0).astype(jnp.bfloat16)
                product = lax.dot_general(
                    factor_u, leaf[:, half:], (((1,), (1,)), ((), ())), preferred_element_type=jnp.float32
                )
                dense = jnp.where(near, leaf.astype(jnp.float32), product).astype(jnp.bfloat16)
                start = (which * leaf_rows + row) * block
                dense_ref[start : start + block, col * block : (col + 1) * block] = dense


def join_kernel(mine_ref, theirs_ref, *outs):
    half = mine_ref.shape[1] // 2
    side = lax.axis_index("src") % 2
    theirs = pltpu.roll(theirs_ref[...], half, 1)
    joined = jnp.where(lane_side(theirs.shape, half) == side, mine_ref[...], theirs)
    each = joined.shape[0] // len(outs)
    for i, out in enumerate(outs):
        out[...] = joined[i * each : (i + 1) * each]


def unpack_kernel(count, *refs):
    blocks, outs, dev_ref = refs[: -count - 1], refs[-count - 1 : -1], refs[-1]
    own = blocks[0].shape[0] // count
    far = lax.axis_index("src") // 2
    for step, block in enumerate(blocks):
        start = pl.multiple_of(origin(far, step, len(blocks)) * own, own)
        for i, out in enumerate(outs):
            out[pl.ds(start, own)] = block[i * own : (i + 1) * own]
    dev_ref[...] = deviation_of(friction(*(out[...] for out in outs[:4])))


def stage_kernel(stage, own, dense_count, targets, *refs):
    refs, all_dev = refs[:-1], refs[-1]
    dense_in, refs = refs[:dense_count], refs[dense_count:]
    dev_in, refs = refs[:targets], refs[targets:]
    begin_in, (a_ref, h_ref), refs = refs[:3], refs[3:5], refs[5:]
    now_in, outs = (refs[:3], refs[3:]) if stage else (begin_in, refs)

    joined, members = dev_in[0].shape
    half = members // 2
    rows, line = 2 * joined, joined // own
    for step, dev_ref in enumerate(dev_in):
        place = origin(lax.axis_index("tgt"), step, targets) * rows
        dev = dev_ref[...].astype(jnp.float32)
        for side, part in enumerate((dev, pltpu.roll(dev, half, 1))):
            for far in range(line):
                start = pl.multiple_of(place + (2 * far + side) * own, own)
                all_dev[pl.ds(start, own)] = part[far * own : (far + 1) * own]
    deviations = all_dev[...].astype(jnp.bfloat16)
    if stage == 0:
        dense_ref, outs = outs[-1], outs[:-1]
        width = dense_in[0].shape[1]
        for place, dense in zip(block_order(lax.axis_index("src"), dense_count), dense_in):
            dense_ref[:, pl.ds(pl.multiple_of(place * width, width), width)] = dense[...]
    else:
        dense_ref = dense_in[0]

    if stage < 2:
        mine, kept = slice(None), line
        total = jnp.dot(dense_ref[...], deviations, preferred_element_type=jnp.float32)
        totals = [total[:rows], total[rows:]]
    else:
        kept = 1
        far = lax.axis_index("src") // 2
        mine = pl.ds(pl.multiple_of(far * own, own), own)
        start = pl.multiple_of(far * 2 * own, 2 * own)
        totals = [
            jnp.dot(dense_ref[pl.ds(first + start, 2 * own)], deviations, preferred_element_type=jnp.float32)
            for first in (0, rows)
        ]
    change = []
    for total in totals:
        sides = [
            jnp.concatenate([total[(2 * far + side) * own : (2 * far + side + 1) * own] for far in range(kept)])
            for side in range(2)
        ]
        change.append(
            jnp.where(lane_side(sides[0].shape, half) == 0, sides[0], pltpu.roll(sides[1], half, 1))
        )
    now = tuple(ref[mine] for ref in now_in)
    friction_a = a_ref[mine]
    change.append(h_ref[mine] * (jnp.exp(-now[2]) - friction(*now, friction_a)))
    moved = tuple(value + time_step * rate for value, rate in zip(now, change))
    if stage:
        begin = tuple(ref[mine] for ref in begin_in)
    if stage == 1:
        moved = tuple(0.75 * first + 0.25 * value for first, value in zip(begin, moved))
    elif stage == 2:
        moved = tuple(first / 3.0 + (2.0 / 3.0) * value for first, value in zip(begin, moved))
        for i, value in enumerate(moved):
            outs[0][i * own : (i + 1) * own] = value
        return
    for out, value in zip(outs, moved):
        out[...] = value
    outs[3][...] = deviation_of(friction(*moved, friction_a))


def call(kernel, outs, given, scratch=(), space=VMEM):
    return pl.pallas_call(
        kernel,
        out_shape=tuple(outs),
        in_specs=[space] * len(given),
        out_specs=(VMEM,) * len(outs),
        scratch_shapes=list(scratch),
        compiler_params=pltpu.CompilerParams(vmem_limit_bytes=32 << 20),
    )(*given)


def per_device(
    shear_leaves, normal_leaves, near_flags, ranks, shear_traction, normal_traction, state, friction_a, heal_rate
):
    leaf_rows, leaf_cols, block, _ = shear_leaves.shape
    own, members = state.shape
    sources, targets = lax.axis_size("src"), lax.axis_size("tgt")
    rows = own * sources
    arrays = (shear_traction, normal_traction, state, friction_a, heal_rate)

    def floats(count):
        return jax.ShapeDtypeStruct((count, members), jnp.float32)

    wide = floats(rows // 2)
    dev_type = jax.ShapeDtypeStruct((rows // 2, members), jnp.bfloat16)

    given = (near_flags.T, ranks.T, shear_leaves, normal_leaves, *arrays)
    given = tuple(pltpu.with_memory_space_constraint(value, pltpu.HBM) for value in given)
    packed, dense = call(
        prepare_kernel,
        (floats(len(arrays) * own), jax.ShapeDtypeStruct((2 * rows, leaf_cols * block), jnp.bfloat16)),
        given,
        [pltpu.VMEM(value.shape, value.dtype) for value in given[:4]] + [pltpu.SemaphoreType.DMA((len(given),))],
        HBM,
    )
    (joined,) = call(join_kernel, (floats(len(arrays) * own),), (packed, across_pair(packed)))
    joined_blocks = gather_line(joined)
    other = across_pair(dense)
    held = gather_line(dense, (other,))
    dense_blocks = held + [other] + [across_pair(value) for value in held[1:]]
    *begin, all_a, all_h, dev = call(
        functools.partial(unpack_kernel, len(arrays)), (wide,) * len(arrays) + (dev_type,), joined_blocks
    )
    now = ()
    matrix_type = jax.ShapeDtypeStruct((2 * rows, sources * leaf_cols * block), jnp.bfloat16)
    for stage in range(3):
        given = (*dense_blocks, *gather_target(dev), *begin, all_a, all_h, *now)
        outs = ((wide,) * 3 + (dev_type,)) if stage < 2 else (floats(3 * own),)
        outs = outs + ((matrix_type,) if stage == 0 else ())
        results = call(
            functools.partial(stage_kernel, stage, own, len(dense_blocks), targets),
            outs,
            given,
            [pltpu.VMEM((rows * targets, members), jnp.float32)],
        )
        now = results[:3]
        if stage < 2:
            dev = results[3]
        if stage == 0:
            dense_blocks = [results[4]]
    return call(join_kernel, (floats(own),) * 3, (results[0], across_pair(results[0])))


def solution(mesh):
    rows = P(("tgt", "src"), None)
    leaves = P("tgt", "src", None, None)
    flags = P("tgt", "src")
    return jax.shard_map(
        per_device,
        mesh=mesh,
        in_specs=(leaves, leaves, flags, flags) + (rows,) * 5,
        out_specs=(rows,) * 3,
        check_vma=False,
    )
```

```python
import functools

import jax
import jax.numpy as jnp
from jax import lax
from jax.experimental import pallas as pl
from jax.experimental.pallas import tpu as pltpu
from jax.sharding import PartitionSpec as P

time_step = 0.25
PAIR = 2
VMEM = pl.BlockSpec(memory_space=pltpu.VMEM)
HBM = pl.BlockSpec(memory_space=pltpu.HBM)


def partner(index, step, count):
    return index ^ step if count & (count - 1) == 0 else (index + step) % count


def origin(index, step, count):
    return index ^ step if count & (count - 1) == 0 else (index + count - step) % count


def block_order(me, sources):
    line = sources // PAIR
    return [origin(me // PAIR, step, line) * PAIR + (me % PAIR ^ side) for side in range(PAIR) for step in range(line)]


def along_line(block, step):
    sources = lax.axis_size("src")
    moves = [(i, partner(i // PAIR, step, sources // PAIR) * PAIR + i % PAIR) for i in range(sources)]
    return lax.ppermute(block, "src", moves)


def across_pair(block):
    return lax.ppermute(block, "src", [(i, i ^ 1) for i in range(lax.axis_size("src"))])


def gather_line(block, ready=()):
    line = lax.axis_size("src") // PAIR
    blocks = [block]
    for step in range(1, line):
        low = step & -step
        if line & (line - 1) or step == low:
            blocks.append(along_line(block, step))
        else:
            held, *_ = lax.optimization_barrier((blocks[step ^ low], *ready))
            blocks.append(along_line(held, low))
    return blocks


def gather_target(block):
    targets = lax.axis_size("tgt")
    return [block] + [
        lax.ppermute(block, "tgt", [(i, partner(i, step, targets)) for i in range(targets)])
        for step in range(1, targets)
    ]


def friction(shear_now, normal_now, state_now, friction_a):
    drive = shear_now / (friction_a * jnp.maximum(normal_now, 1.0))
    decay = state_now / friction_a
    return jnp.exp(drive - decay) - jnp.exp(-drive - decay)


def deviation_of(slip_rate):
    return (slip_rate - 1.0).astype(jnp.bfloat16)


def lane_side(shape, half):
    return lax.broadcasted_iota(jnp.int32, shape, len(shape) - 1) // half


def prepare_kernel(*refs):
    given, (packed_ref, dense_ref), held, sems = refs[:9], refs[9:11], refs[11:15], refs[15]
    own = given[4].shape[0]
    copies = [pltpu.make_async_copy(ref, place, sems.at[i]) for i, (ref, place) in enumerate(zip(given, held))]
    copies += [
        pltpu.make_async_copy(ref, packed_ref.at[pl.ds(i * own, own)], sems.at[4 + i])
        for i, ref in enumerate(given[4:])
    ]
    for copy in copies:
        copy.start()
    for copy in copies:
        copy.wait()
    near_ref, rank_ref, shear_ref, normal_ref = held
    leaf_rows, leaf_cols, block, _ = shear_ref.shape
    half = block // 2
    rank_ids = lax.broadcasted_iota(jnp.int32, (block, half), 1)
    for which, leaves in enumerate((shear_ref, normal_ref)):
        for row in range(leaf_rows):
            for col in range(leaf_cols):
                near = near_ref[col : col + 1, row : row + 1] == 1
                leaf = leaves[row, col]
                kept = rank_ids < rank_ref[col : col + 1, row : row + 1]
                factor_u = jnp.where(kept, leaf[:, :half].astype(jnp.float32), 0.0).astype(jnp.bfloat16)
                product = lax.dot_general(
                    factor_u, leaf[:, half:], (((1,), (1,)), ((), ())), preferred_element_type=jnp.float32
                )
                dense = jnp.where(near, leaf.astype(jnp.float32), product).astype(jnp.bfloat16)
                start = (which * leaf_rows + row) * block
                dense_ref[start : start + block, col * block : (col + 1) * block] = dense


def join_kernel(mine_ref, theirs_ref, *outs):
    half = mine_ref.shape[1] // 2
    side = lax.axis_index("src") % 2
    theirs = pltpu.roll(theirs_ref[...], half, 1)
    joined = jnp.where(lane_side(theirs.shape, half) == side, mine_ref[...], theirs)
    each = joined.shape[0] // len(outs)
    for i, out in enumerate(outs):
        out[...] = joined[i * each : (i + 1) * each]


def unpack_kernel(count, *refs):
    blocks, outs, (dev_ref, slips) = refs[: -count - 2], refs[-count - 2 : -2], refs[-2:]
    blocks, slips_in = blocks[: len(blocks) // 2], blocks[len(blocks) // 2 :]
    own = blocks[0].shape[0] // count
    far = lax.axis_index("src") // 2
    for step, (block, slip_in) in enumerate(zip(blocks, slips_in)):
        start = pl.multiple_of(origin(far, step, len(blocks)) * own, own)
        slips[pl.ds(start, own)] = slip_in[...]
        for i, out in enumerate(outs):
            out[pl.ds(start, own)] = block[i * own : (i + 1) * own]
    dev_ref[...] = deviation_of(slips[...])


def stage_kernel(stage, own, dense_count, targets, *refs):
    refs, all_dev = refs[:-1], refs[-1]
    dense_in, refs = refs[:dense_count], refs[dense_count:]
    dev_in, refs = refs[:targets], refs[targets:]
    begin_in, (a_ref, h_ref), refs = refs[:3], refs[3:5], refs[5:]
    now_in, outs = (refs[:3], refs[3:]) if stage else (begin_in, refs)

    joined, members = dev_in[0].shape
    half = members // 2
    rows, line = 2 * joined, joined // own
    for step, dev_ref in enumerate(dev_in):
        place = origin(lax.axis_index("tgt"), step, targets) * rows
        dev = dev_ref[...].astype(jnp.float32)
        for side, part in enumerate((dev, pltpu.roll(dev, half, 1))):
            for far in range(line):
                start = pl.multiple_of(place + (2 * far + side) * own, own)
                all_dev[pl.ds(start, own)] = part[far * own : (far + 1) * own]
    deviations = all_dev[...].astype(jnp.bfloat16)
    if stage == 0:
        dense_ref, outs = outs[-1], outs[:-1]
        width = dense_in[0].shape[1]
        for place, dense in zip(block_order(lax.axis_index("src"), dense_count), dense_in):
            dense_ref[:, pl.ds(pl.multiple_of(place * width, width), width)] = dense[...]
    else:
        dense_ref = dense_in[0]

    if stage < 2:
        mine, kept = slice(None), line
        total = jnp.dot(dense_ref[...], deviations, preferred_element_type=jnp.float32)
        totals = [total[:rows], total[rows:]]
    else:
        kept = 1
        far = lax.axis_index("src") // 2
        mine = pl.ds(pl.multiple_of(far * own, own), own)
        start = pl.multiple_of(far * 2 * own, 2 * own)
        totals = [
            jnp.dot(dense_ref[pl.ds(first + start, 2 * own)], deviations, preferred_element_type=jnp.float32)
            for first in (0, rows)
        ]
    change = []
    for total in totals:
        sides = [
            jnp.concatenate([total[(2 * far + side) * own : (2 * far + side + 1) * own] for far in range(kept)])
            for side in range(2)
        ]
        change.append(
            jnp.where(lane_side(sides[0].shape, half) == 0, sides[0], pltpu.roll(sides[1], half, 1))
        )
    now = tuple(ref[mine] for ref in now_in)
    friction_a = a_ref[mine]
    change.append(h_ref[mine] * (jnp.exp(-now[2]) - friction(*now, friction_a)))
    moved = tuple(value + time_step * rate for value, rate in zip(now, change))
    if stage:
        begin = tuple(ref[mine] for ref in begin_in)
    if stage == 1:
        moved = tuple(0.75 * first + 0.25 * value for first, value in zip(begin, moved))
    elif stage == 2:
        moved = tuple(first / 3.0 + (2.0 / 3.0) * value for first, value in zip(begin, moved))
        for i, value in enumerate(moved):
            outs[0][i * own : (i + 1) * own] = value
        return
    for out, value in zip(outs, moved):
        out[...] = value
    outs[3][...] = deviation_of(friction(*moved, friction_a))


def call(kernel, outs, given, scratch=(), space=VMEM):
    return pl.pallas_call(
        kernel,
        out_shape=tuple(outs),
        in_specs=[space] * len(given),
        out_specs=(VMEM,) * len(outs),
        scratch_shapes=list(scratch),
        compiler_params=pltpu.CompilerParams(vmem_limit_bytes=32 << 20),
    )(*given)


def per_device(
    shear_leaves, normal_leaves, near_flags, ranks, shear_traction, normal_traction, state, friction_a, heal_rate
):
    leaf_rows, leaf_cols, block, _ = shear_leaves.shape
    own, members = state.shape
    sources, targets = lax.axis_size("src"), lax.axis_size("tgt")
    rows = own * sources
    arrays = (shear_traction, normal_traction, state, friction_a, heal_rate)

    def floats(count):
        return jax.ShapeDtypeStruct((count, members), jnp.float32)

    wide = floats(rows // 2)
    dev_type = jax.ShapeDtypeStruct((rows // 2, members), jnp.bfloat16)

    given = (near_flags.T, ranks.T, shear_leaves, normal_leaves, *arrays)
    given = tuple(pltpu.with_memory_space_constraint(value, pltpu.HBM) for value in given)
    packed, dense = call(
        prepare_kernel,
        (floats(len(arrays) * own), jax.ShapeDtypeStruct((2 * rows, leaf_cols * block), jnp.bfloat16)),
        given,
        [pltpu.VMEM(value.shape, value.dtype) for value in given[:4]] + [pltpu.SemaphoreType.DMA((len(given),))],
        HBM,
    )
    (joined,) = call(join_kernel, (floats(len(arrays) * own),), (packed, across_pair(packed)))
    joined_blocks = gather_line(joined)
    first_slips = [friction(*jnp.split(value, len(arrays))[:4]) for value in joined_blocks]
    other = across_pair(dense)
    held = gather_line(dense, (other,))
    dense_blocks = held + [other] + [across_pair(value) for value in held[1:]]
    *begin, all_a, all_h, dev = call(
        functools.partial(unpack_kernel, len(arrays)),
        (wide,) * len(arrays) + (dev_type,),
        joined_blocks + first_slips,
        [pltpu.VMEM(wide.shape, wide.dtype)],
    )
    now = ()
    matrix_type = jax.ShapeDtypeStruct((2 * rows, sources * leaf_cols * block), jnp.bfloat16)
    for stage in range(3):
        given = (*dense_blocks, *gather_target(dev), *begin, all_a, all_h, *now)
        outs = ((wide,) * 3 + (dev_type,)) if stage < 2 else (floats(3 * own),)
        outs = outs + ((matrix_type,) if stage == 0 else ())
        results = call(
            functools.partial(stage_kernel, stage, own, len(dense_blocks), targets),
            outs,
            given,
            [pltpu.VMEM((rows * targets, members), jnp.float32)],
        )
        now = results[:3]
        if stage < 2:
            dev = results[3]
        if stage == 0:
            dense_blocks = [results[4]]
    return call(join_kernel, (floats(own),) * 3, (results[0], across_pair(results[0])))


def solution(mesh):
    rows = P(("tgt", "src"), None)
    leaves = P("tgt", "src", None, None)
    flags = P("tgt", "src")
    return jax.shard_map(
        per_device,
        mesh=mesh,
        in_specs=(leaves, leaves, flags, flags) + (rows,) * 5,
        out_specs=(rows,) * 3,
        check_vma=False,
    )
```

```python
import functools

import jax
import jax.numpy as jnp
from jax import lax
from jax.experimental import pallas as pl
from jax.experimental.pallas import tpu as pltpu
from jax.sharding import PartitionSpec as P

time_step = 0.25
PAIR = 2
VMEM = pl.BlockSpec(memory_space=pltpu.VMEM)
HBM = pl.BlockSpec(memory_space=pltpu.HBM)


def partner(index, step, count):
    return index ^ step if count & (count - 1) == 0 else (index + step) % count


def origin(index, step, count):
    return index ^ step if count & (count - 1) == 0 else (index + count - step) % count


def block_order(me, sources):
    line = sources // PAIR
    return [origin(me // PAIR, step, line) * PAIR + (me % PAIR ^ side) for side in range(PAIR) for step in range(line)]


def along_line(block, step):
    sources = lax.axis_size("src")
    moves = [(i, partner(i // PAIR, step, sources // PAIR) * PAIR + i % PAIR) for i in range(sources)]
    return lax.ppermute(block, "src", moves)


def across_pair(block):
    return lax.ppermute(block, "src", [(i, i ^ 1) for i in range(lax.axis_size("src"))])


def gather_line(block, ready=()):
    line = lax.axis_size("src") // PAIR
    blocks = [block]
    for step in range(1, line):
        low = step & -step
        if line & (line - 1) or step == low:
            blocks.append(along_line(block, step))
        else:
            held, *_ = lax.optimization_barrier((blocks[step ^ low], *ready))
            blocks.append(along_line(held, low))
    return blocks


def gather_target(block):
    targets = lax.axis_size("tgt")
    return [block] + [
        lax.ppermute(block, "tgt", [(i, partner(i, step, targets)) for i in range(targets)])
        for step in range(1, targets)
    ]


def friction(shear_now, normal_now, state_now, friction_a):
    drive = shear_now / (friction_a * jnp.maximum(normal_now, 1.0))
    decay = state_now / friction_a
    return jnp.exp(drive - decay) - jnp.exp(-drive - decay)


def deviation_of(slip_rate):
    return (slip_rate - 1.0).astype(jnp.bfloat16)


def lane_side(shape, half):
    return lax.broadcasted_iota(jnp.int32, shape, len(shape) - 1) // half


def prepare_kernel(*refs):
    given, (packed_ref, dense_ref), held, sems = refs[:9], refs[9:11], refs[11:15], refs[15]
    own = given[4].shape[0]
    copies = [pltpu.make_async_copy(ref, place, sems.at[i]) for i, (ref, place) in enumerate(zip(given, held))]
    copies += [
        pltpu.make_async_copy(ref, packed_ref.at[pl.ds(i * own, own)], sems.at[4 + i])
        for i, ref in enumerate(given[4:])
    ]
    for copy in copies:
        copy.start()
    for copy in copies:
        copy.wait()
    near_ref, rank_ref, shear_ref, normal_ref = held
    leaf_rows, leaf_cols, block, _ = shear_ref.shape
    half = block // 2
    rank_ids = lax.broadcasted_iota(jnp.int32, (block, half), 1)
    for which, leaves in enumerate((shear_ref, normal_ref)):
        for row in range(leaf_rows):
            for col in range(leaf_cols):
                near = near_ref[col : col + 1, row : row + 1] == 1
                leaf = leaves[row, col]
                kept = rank_ids < rank_ref[col : col + 1, row : row + 1]
                factor_u = jnp.where(kept, leaf[:, :half].astype(jnp.float32), 0.0).astype(jnp.bfloat16)
                product = lax.dot_general(
                    factor_u, leaf[:, half:], (((1,), (1,)), ((), ())), preferred_element_type=jnp.float32
                )
                dense = jnp.where(near, leaf.astype(jnp.float32), product).astype(jnp.bfloat16)
                start = (which * leaf_rows + row) * block
                dense_ref[start : start + block, col * block : (col + 1) * block] = dense


def join_kernel(mine_ref, theirs_ref, joined_ref):
    half = mine_ref.shape[1] // 2
    side = lax.axis_index("src") % PAIR
    theirs = pltpu.roll(theirs_ref[...], half, 1)
    joined_ref[...] = jnp.where(lane_side(theirs.shape, half) == side, mine_ref[...], theirs)


def fold(value, side):
    rows, half = value.shape[0] // 2, value.shape[1] // 2
    moved = pltpu.roll(value, half, 1)
    left = jnp.where(side == 0, value[:rows], moved[:rows])
    right = jnp.where(side == 0, moved[rows:], value[rows:])
    return jnp.where(lane_side(left.shape, half) == 0, left, right)


def finish_kernel(mine_ref, theirs_ref, *outs):
    half = mine_ref.shape[1] // 2
    side = lax.axis_index("src") % PAIR
    theirs = theirs_ref[...]
    moved = pltpu.roll(theirs, half, 1)
    theirs = jnp.concatenate([jnp.where(side == 1, theirs, moved), jnp.where(side == 1, moved, theirs)])
    done = jnp.where(lane_side(theirs.shape, half) == side, mine_ref[...], theirs)
    own = done.shape[0] // len(outs)
    for i, out in enumerate(outs):
        out[...] = done[i * own : (i + 1) * own]


def unpack_kernel(count, *refs):
    blocks, outs, (dev_ref, slips) = refs[: -count - 2], refs[-count - 2 : -2], refs[-2:]
    blocks, slips_in = blocks[: len(blocks) // 2], blocks[len(blocks) // 2 :]
    own = blocks[0].shape[0] // count
    far = lax.axis_index("src") // 2
    for step, (block, slip_in) in enumerate(zip(blocks, slips_in)):
        start = pl.multiple_of(origin(far, step, len(blocks)) * own, own)
        slips[pl.ds(start, own)] = slip_in[...]
        for i, out in enumerate(outs):
            out[pl.ds(start, own)] = block[i * own : (i + 1) * own]
    dev_ref[...] = deviation_of(slips[...])


def stage_kernel(stage, own, dense_count, targets, *refs):
    refs, all_dev = refs[:-1], refs[-1]
    dense_in, refs = refs[:dense_count], refs[dense_count:]
    dev_in, refs = refs[:targets], refs[targets:]
    begin_in, (a_ref, h_ref), refs = refs[:3], refs[3:5], refs[5:]
    now_in, outs = (refs[:3], refs[3:]) if stage else (begin_in, refs)

    joined, members = dev_in[0].shape
    half = members // 2
    rows, line = 2 * joined, joined // own
    for step, dev_ref in enumerate(dev_in):
        place = origin(lax.axis_index("tgt"), step, targets) * rows
        dev = dev_ref[...].astype(jnp.float32)
        for side, part in enumerate((dev, pltpu.roll(dev, half, 1))):
            for far in range(line):
                start = pl.multiple_of(place + (2 * far + side) * own, own)
                all_dev[pl.ds(start, own)] = part[far * own : (far + 1) * own]
    deviations = all_dev[...].astype(jnp.bfloat16)
    if stage == 0:
        dense_ref, outs = outs[-1], outs[:-1]
        width = dense_in[0].shape[1]
        for place, dense in zip(block_order(lax.axis_index("src"), dense_count), dense_in):
            dense_ref[:, pl.ds(pl.multiple_of(place * width, width), width)] = dense[...]
    else:
        dense_ref = dense_in[0]

    if stage < 2:
        mine, kept = slice(None), line
        total = jnp.dot(dense_ref[...], deviations, preferred_element_type=jnp.float32)
        totals = [total[:rows], total[rows:]]
    else:
        kept = 1
        far = lax.axis_index("src") // 2
        mine = pl.ds(pl.multiple_of(far * own, own), own)
        start = pl.multiple_of(far * 2 * own, 2 * own)
        totals = [
            jnp.dot(dense_ref[pl.ds(first + start, 2 * own)], deviations, preferred_element_type=jnp.float32)
            for first in (0, rows)
        ]
    change = []
    for total in totals:
        sides = [
            jnp.concatenate([total[(2 * far + side) * own : (2 * far + side + 1) * own] for far in range(kept)])
            for side in range(2)
        ]
        change.append(
            jnp.where(lane_side(sides[0].shape, half) == 0, sides[0], pltpu.roll(sides[1], half, 1))
        )
    now = tuple(ref[mine] for ref in now_in)
    friction_a = a_ref[mine]
    change.append(h_ref[mine] * (jnp.exp(-now[2]) - friction(*now, friction_a)))
    moved = tuple(value + time_step * rate for value, rate in zip(now, change))
    if stage:
        begin = tuple(ref[mine] for ref in begin_in)
    if stage == 1:
        moved = tuple(0.75 * first + 0.25 * value for first, value in zip(begin, moved))
    elif stage == 2:
        moved = tuple(first / 3.0 + (2.0 / 3.0) * value for first, value in zip(begin, moved))
        done = jnp.concatenate(moved)
        outs[0][...] = done
        outs[1][...] = fold(done, 1 - lax.axis_index("src") % PAIR)
        return
    for out, value in zip(outs, moved):
        out[...] = value
    outs[3][...] = deviation_of(friction(*moved, friction_a))


def call(kernel, outs, given, scratch=(), space=VMEM):
    return pl.pallas_call(
        kernel,
        out_shape=tuple(outs),
        in_specs=[space] * len(given),
        out_specs=(VMEM,) * len(outs),
        scratch_shapes=list(scratch),
        compiler_params=pltpu.CompilerParams(vmem_limit_bytes=32 << 20),
    )(*given)


def per_device(
    shear_leaves, normal_leaves, near_flags, ranks, shear_traction, normal_traction, state, friction_a, heal_rate
):
    leaf_rows, leaf_cols, block, _ = shear_leaves.shape
    own, members = state.shape
    sources, targets = lax.axis_size("src"), lax.axis_size("tgt")
    rows = own * sources
    arrays = (shear_traction, normal_traction, state, friction_a, heal_rate)

    def floats(count):
        return jax.ShapeDtypeStruct((count, members), jnp.float32)

    wide = floats(rows // 2)
    dev_type = jax.ShapeDtypeStruct((rows // 2, members), jnp.bfloat16)

    given = (near_flags.T, ranks.T, shear_leaves, normal_leaves, *arrays)
    given = tuple(pltpu.with_memory_space_constraint(value, pltpu.HBM) for value in given)
    packed, dense = call(
        prepare_kernel,
        (floats(len(arrays) * own), jax.ShapeDtypeStruct((2 * rows, leaf_cols * block), jnp.bfloat16)),
        given,
        [pltpu.VMEM(value.shape, value.dtype) for value in given[:4]] + [pltpu.SemaphoreType.DMA((len(given),))],
        HBM,
    )
    (joined,) = call(join_kernel, (floats(len(arrays) * own),), (packed, across_pair(packed)))
    joined_blocks = gather_line(joined)
    first_slips = [friction(*jnp.split(value, len(arrays))[:4]) for value in joined_blocks]
    other = across_pair(dense)
    held = gather_line(dense, (other,))
    dense_blocks = held + [other] + [across_pair(value) for value in held[1:]]
    *begin, all_a, all_h, dev = call(
        functools.partial(unpack_kernel, len(arrays)),
        (wide,) * len(arrays) + (dev_type,),
        joined_blocks + first_slips,
        [pltpu.VMEM(wide.shape, wide.dtype)],
    )
    now = ()
    matrix_type = jax.ShapeDtypeStruct((2 * rows, sources * leaf_cols * block), jnp.bfloat16)
    for stage in range(3):
        given = (*dense_blocks, *gather_target(dev), *begin, all_a, all_h, *now)
        outs = ((wide,) * 3 + (dev_type,)) if stage < 2 else (floats(3 * own), floats(3 * own // 2))
        outs = outs + ((matrix_type,) if stage == 0 else ())
        results = call(
            functools.partial(stage_kernel, stage, own, len(dense_blocks), targets),
            outs,
            given,
            [pltpu.VMEM((rows * targets, members), jnp.float32)],
        )
        now = results[:3]
        if stage < 2:
            dev = results[3]
        if stage == 0:
            dense_blocks = [results[4]]
    return call(finish_kernel, (floats(own),) * 3, (results[0], across_pair(results[1])))


def solution(mesh):
    rows = P(("tgt", "src"), None)
    leaves = P("tgt", "src", None, None)
    flags = P("tgt", "src")
    return jax.shard_map(
        per_device,
        mesh=mesh,
        in_specs=(leaves, leaves, flags, flags) + (rows,) * 5,
        out_specs=(rows,) * 3,
        check_vma=False,
    )
```

```python
import functools

import jax
import jax.numpy as jnp
from jax import lax
from jax.experimental import pallas as pl
from jax.experimental.pallas import tpu as pltpu
from jax.sharding import PartitionSpec as P

time_step = 0.25
PAIR = 2
EARLY = 1
VMEM = pl.BlockSpec(memory_space=pltpu.VMEM)
HBM = pl.BlockSpec(memory_space=pltpu.HBM)


def partner(index, step, count):
    return index ^ step if count & (count - 1) == 0 else (index + step) % count


def origin(index, step, count):
    return index ^ step if count & (count - 1) == 0 else (index + count - step) % count


def block_order(me, sources):
    line = sources // PAIR
    return [origin(me // PAIR, step, line) * PAIR + (me % PAIR ^ side) for side in range(PAIR) for step in range(line)]


def along_line(block, step):
    sources = lax.axis_size("src")
    moves = [(i, partner(i // PAIR, step, sources // PAIR) * PAIR + i % PAIR) for i in range(sources)]
    return lax.ppermute(block, "src", moves)


def across_pair(block):
    return lax.ppermute(block, "src", [(i, i ^ 1) for i in range(lax.axis_size("src"))])


def gather_line(block, ready=()):
    line = lax.axis_size("src") // PAIR
    blocks = [block]
    for step in range(1, line):
        low = step & -step
        if line & (line - 1) or step == low:
            blocks.append(along_line(block, step))
        else:
            held, *_ = lax.optimization_barrier((blocks[step ^ low], *ready))
            blocks.append(along_line(held, low))
    return blocks


def gather_target(block):
    targets = lax.axis_size("tgt")
    return [block] + [
        lax.ppermute(block, "tgt", [(i, partner(i, step, targets)) for i in range(targets)])
        for step in range(1, targets)
    ]


def friction(shear_now, normal_now, state_now, friction_a):
    drive = shear_now / (friction_a * jnp.maximum(normal_now, 1.0))
    decay = state_now / friction_a
    return jnp.exp(drive - decay) - jnp.exp(-drive - decay)


def deviation_of(slip_rate):
    return (slip_rate - 1.0).astype(jnp.bfloat16)


def lane_side(shape, half):
    return lax.broadcasted_iota(jnp.int32, shape, len(shape) - 1) // half


def prepare_kernel(*refs):
    given, (packed_ref, dense_ref), held, sems = refs[:9], refs[9:11], refs[11:15], refs[15]
    own = given[4].shape[0]
    copies = [pltpu.make_async_copy(ref, place, sems.at[i]) for i, (ref, place) in enumerate(zip(given, held))]
    copies += [
        pltpu.make_async_copy(ref, packed_ref.at[pl.ds(i * own, own)], sems.at[4 + i])
        for i, ref in enumerate(given[4:])
    ]
    for copy in copies:
        copy.start()
    for copy in copies:
        copy.wait()
    near_ref, rank_ref, shear_ref, normal_ref = held
    leaf_rows, leaf_cols, block, _ = shear_ref.shape
    half = block // 2
    rank_ids = lax.broadcasted_iota(jnp.int32, (block, half), 1)
    for which, leaves in enumerate((shear_ref, normal_ref)):
        for row in range(leaf_rows):
            for col in range(leaf_cols):
                near = near_ref[col : col + 1, row : row + 1] == 1
                leaf = leaves[row, col]
                kept = rank_ids < rank_ref[col : col + 1, row : row + 1]
                factor_u = jnp.where(kept, leaf[:, :half].astype(jnp.float32), 0.0).astype(jnp.bfloat16)
                product = lax.dot_general(
                    factor_u, leaf[:, half:], (((1,), (1,)), ((), ())), preferred_element_type=jnp.float32
                )
                dense = jnp.where(near, leaf.astype(jnp.float32), product).astype(jnp.bfloat16)
                start = (which * leaf_rows + row) * block
                dense_ref[start : start + block, col * block : (col + 1) * block] = dense


def join_kernel(mine_ref, theirs_ref, joined_ref):
    half = mine_ref.shape[1] // 2
    side = lax.axis_index("src") % PAIR
    theirs = pltpu.roll(theirs_ref[...], half, 1)
    joined_ref[...] = jnp.where(lane_side(theirs.shape, half) == side, mine_ref[...], theirs)


def fold(value, side):
    rows, half = value.shape[0] // 2, value.shape[1] // 2
    moved = pltpu.roll(value, half, 1)
    left = jnp.where(side == 0, value[:rows], moved[:rows])
    right = jnp.where(side == 0, moved[rows:], value[rows:])
    return jnp.where(lane_side(left.shape, half) == 0, left, right)


def finish_kernel(mine_ref, theirs_ref, *outs):
    half = mine_ref.shape[1] // 2
    side = lax.axis_index("src") % PAIR
    theirs = theirs_ref[...]
    moved = pltpu.roll(theirs, half, 1)
    theirs = jnp.concatenate([jnp.where(side == 1, theirs, moved), jnp.where(side == 1, moved, theirs)])
    done = jnp.where(lane_side(theirs.shape, half) == side, mine_ref[...], theirs)
    own = done.shape[0] // len(outs)
    for i, out in enumerate(outs):
        out[...] = done[i * own : (i + 1) * own]


def unpack_kernel(count, *refs):
    blocks, outs, (dev_ref, slips) = refs[: -count - 2], refs[-count - 2 : -2], refs[-2:]
    blocks, slips_in = blocks[: len(blocks) // 2], blocks[len(blocks) // 2 :]
    own = blocks[0].shape[0] // count
    far = lax.axis_index("src") // 2
    for step, (block, slip_in) in enumerate(zip(blocks, slips_in)):
        start = pl.multiple_of(origin(far, step, len(blocks)) * own, own)
        slips[pl.ds(start, own)] = slip_in[...]
        for i, out in enumerate(outs):
            out[pl.ds(start, own)] = block[i * own : (i + 1) * own]
    dev_ref[...] = deviation_of(slips[...])


def place_deviations(dev_ref, place, own, scratch):
    dev = dev_ref[...].astype(jnp.float32)
    half = dev.shape[1] // 2
    for side, part in enumerate((dev, pltpu.roll(dev, half, 1))):
        for far in range(dev.shape[0] // own):
            start = pl.multiple_of(place + (2 * far + side) * own, own)
            scratch[pl.ds(start, own)] = part[far * own : (far + 1) * own]


def product(stage, own, steps, targets, dense_ref, dev_refs, scratch):
    rows = 2 * dev_refs[0].shape[0]
    start = pl.multiple_of(lax.axis_index("src") // PAIR * 2 * own, 2 * own)
    total = 0.0
    for i, (step, dev_ref) in enumerate(zip(steps, dev_refs)):
        place_deviations(dev_ref, i * rows, own, scratch)
        columns = pl.ds(pl.multiple_of(origin(lax.axis_index("tgt"), step, targets) * rows, rows), rows)
        block = scratch[i * rows : (i + 1) * rows].astype(jnp.bfloat16)
        if stage < 2:
            dense = dense_ref[:, columns]
        else:
            dense = jnp.concatenate([dense_ref[pl.ds(first + start, 2 * own), columns] for first in (0, rows)])
        total += jnp.dot(dense, block, preferred_element_type=jnp.float32)
    return total


def early_kernel(stage, own, targets, dense_ref, *refs):
    refs, total_ref, scratch = refs[:-2], refs[-2], refs[-1]
    total_ref[...] = product(stage, own, range(len(refs)), targets, dense_ref, refs, scratch)


def stage_kernel(stage, own, dense_count, targets, *refs):
    refs, all_dev = refs[:-1], refs[-1]
    dense_in, refs = refs[:dense_count], refs[dense_count:]
    late = targets - EARLY if stage else targets
    dev_in, refs = refs[:late], refs[late:]
    if stage:
        early_ref, refs = refs[0], refs[1:]
    begin_in, (a_ref, h_ref), refs = refs[:3], refs[3:5], refs[5:]
    now_in, outs = (refs[:3], refs[3:]) if stage else (begin_in, refs)

    joined, members = dev_in[0].shape
    half = members // 2
    rows, line = 2 * joined, joined // own
    if stage == 0:
        for step, dev_ref in enumerate(dev_in):
            place_deviations(dev_ref, origin(lax.axis_index("tgt"), step, targets) * rows, own, all_dev)
        deviations = all_dev[...].astype(jnp.bfloat16)
        dense_ref, outs = outs[-1], outs[:-1]
        width = dense_in[0].shape[1]
        for place, dense in zip(block_order(lax.axis_index("src"), dense_count), dense_in):
            dense_ref[:, pl.ds(pl.multiple_of(place * width, width), width)] = dense[...]
    else:
        dense_ref = dense_in[0]

    if stage == 0:
        total = jnp.dot(dense_ref[...], deviations, preferred_element_type=jnp.float32)
    else:
        total = early_ref[...] + product(stage, own, range(EARLY, targets), targets, dense_ref, dev_in, all_dev)
    totals = [total[: total.shape[0] // 2], total[total.shape[0] // 2 :]]
    if stage < 2:
        mine, kept = slice(None), line
    else:
        kept = 1
        mine = pl.ds(pl.multiple_of(lax.axis_index("src") // PAIR * own, own), own)
    change = []
    for total in totals:
        sides = [
            jnp.concatenate([total[(2 * far + side) * own : (2 * far + side + 1) * own] for far in range(kept)])
            for side in range(2)
        ]
        change.append(
            jnp.where(lane_side(sides[0].shape, half) == 0, sides[0], pltpu.roll(sides[1], half, 1))
        )
    now = tuple(ref[mine] for ref in now_in)
    friction_a = a_ref[mine]
    change.append(h_ref[mine] * (jnp.exp(-now[2]) - friction(*now, friction_a)))
    moved = tuple(value + time_step * rate for value, rate in zip(now, change))
    if stage:
        begin = tuple(ref[mine] for ref in begin_in)
    if stage == 1:
        moved = tuple(0.75 * first + 0.25 * value for first, value in zip(begin, moved))
    elif stage == 2:
        moved = tuple(first / 3.0 + (2.0 / 3.0) * value for first, value in zip(begin, moved))
        done = jnp.concatenate(moved)
        outs[0][...] = done
        outs[1][...] = fold(done, 1 - lax.axis_index("src") % PAIR)
        return
    for out, value in zip(outs, moved):
        out[...] = value
    outs[3][...] = deviation_of(friction(*moved, friction_a))


def call(kernel, outs, given, scratch=(), space=VMEM):
    return pl.pallas_call(
        kernel,
        out_shape=tuple(outs),
        in_specs=[space] * len(given),
        out_specs=(VMEM,) * len(outs),
        scratch_shapes=list(scratch),
        compiler_params=pltpu.CompilerParams(vmem_limit_bytes=32 << 20),
    )(*given)


def per_device(
    shear_leaves, normal_leaves, near_flags, ranks, shear_traction, normal_traction, state, friction_a, heal_rate
):
    leaf_rows, leaf_cols, block, _ = shear_leaves.shape
    own, members = state.shape
    sources, targets = lax.axis_size("src"), lax.axis_size("tgt")
    rows = own * sources
    arrays = (shear_traction, normal_traction, state, friction_a, heal_rate)

    def floats(count):
        return jax.ShapeDtypeStruct((count, members), jnp.float32)

    wide = floats(rows // 2)
    dev_type = jax.ShapeDtypeStruct((rows // 2, members), jnp.bfloat16)

    given = (near_flags.T, ranks.T, shear_leaves, normal_leaves, *arrays)
    given = tuple(pltpu.with_memory_space_constraint(value, pltpu.HBM) for value in given)
    packed, dense = call(
        prepare_kernel,
        (floats(len(arrays) * own), jax.ShapeDtypeStruct((2 * rows, leaf_cols * block), jnp.bfloat16)),
        given,
        [pltpu.VMEM(value.shape, value.dtype) for value in given[:4]] + [pltpu.SemaphoreType.DMA((len(given),))],
        HBM,
    )
    (joined,) = call(join_kernel, (floats(len(arrays) * own),), (packed, across_pair(packed)))
    joined_blocks = gather_line(joined)
    first_slips = [friction(*jnp.split(value, len(arrays))[:4]) for value in joined_blocks]
    other = across_pair(dense)
    held = gather_line(dense, (other,))
    dense_blocks = held + [other] + [across_pair(value) for value in held[1:]]
    *begin, all_a, all_h, dev = call(
        functools.partial(unpack_kernel, len(arrays)),
        (wide,) * len(arrays) + (dev_type,),
        joined_blocks + first_slips,
        [pltpu.VMEM(wide.shape, wide.dtype)],
    )
    now = ()
    matrix_type = jax.ShapeDtypeStruct((2 * rows, sources * leaf_cols * block), jnp.bfloat16)
    for stage in range(3):
        dev_blocks = gather_target(dev)
        if stage:
            product_rows = 2 * rows if stage < 2 else 4 * own
            early = call(
                functools.partial(early_kernel, stage, own, targets),
                (floats(product_rows),),
                (*dense_blocks, *dev_blocks[:EARLY]),
                [pltpu.VMEM((rows * EARLY, members), jnp.float32)],
            )
            dev_blocks = (*dev_blocks[EARLY:], *early)
        given = (*dense_blocks, *dev_blocks, *begin, all_a, all_h, *now)
        outs = ((wide,) * 3 + (dev_type,)) if stage < 2 else (floats(3 * own), floats(3 * own // 2))
        outs = outs + ((matrix_type,) if stage == 0 else ())
        results = call(
            functools.partial(stage_kernel, stage, own, len(dense_blocks), targets),
            outs,
            given,
            [pltpu.VMEM((rows * targets, members), jnp.float32)],
        )
        now = results[:3]
        if stage < 2:
            dev = results[3]
        if stage == 0:
            dense_blocks = [results[4]]
    return call(finish_kernel, (floats(own),) * 3, (results[0], across_pair(results[1])))


def solution(mesh):
    rows = P(("tgt", "src"), None)
    leaves = P("tgt", "src", None, None)
    flags = P("tgt", "src")
    return jax.shard_map(
        per_device,
        mesh=mesh,
        in_specs=(leaves, leaves, flags, flags) + (rows,) * 5,
        out_specs=(rows,) * 3,
        check_vma=False,
    )
```
